32 devices in a mesh: dp: 8 (over z, x), mp: 4 (over y, core).
Axes of the slice: x: 2, y: 2, z: 4, core: 2. Of those that a mesh axis runs over, the one named last changes fastest.
Arguments:
- inputs: bfloat16 [3072, 8192], P('dp', 'mp'), may hold values from -6 to 6
- gate_preact: bfloat16 [3072, 28672], P('dp', 'mp'), may hold values from -6 to 6
- hidden_grad: bfloat16 [3072, 28672], P('dp', 'mp'), may hold values from -0.15625 to 0.15625
- projector: bfloat16 [8192, 512], P('mp'), may hold values from -0.0625 to 0.0625
- first_moment: float32 [28672, 512], P(('mp', 'dp')), may hold values from -0.6 to 0.6
- second_moment: float32 [28672, 512], P(('mp', 'dp')), may hold values from 0.01 to 0.1
Outputs:
- new_first: float32 [28672, 512], P(('mp', 'dp'))
- new_second: float32 [28672, 512], P(('mp', 'dp'))
- weight_update: bfloat16 [28672, 8192], P(('mp', 'dp'))
The draws below stay inside these ranges and needn't reach their ends.
All inputs are finite; a program needn't handle non-finite values.
Results may differ from the reference program's by a relative error of at most 0.0058.
Values may be sent and summed in bfloat16 or wider, within the bound.
A program may use at most 128 MiB of HBM per device.

```python
import math
import jax
import jax.numpy as jnp

D = 8192
FF = 28672
RANK = 512
TOKENS = 3072


def raised(drawn, stream_key, source, target, parts, factor):
    owner, partner = [(jnp.arange(drawn.shape[dim]) // (drawn.shape[dim] // parts)).reshape([-1 if axis == dim else 1 for axis in range(drawn.ndim)]) for dim in (source, target)]
    chosen = jax.random.permutation(stream_key, parts)[partner]
    strong = (owner == chosen) | (owner == (partner + parts // 2) % parts)
    return jnp.where(strong, factor * drawn, drawn)


def block_levels(rng, shape, cuts, smallest, largest):
    level, own = 1.0, jax.random.fold_in(rng, 6)
    for position, shards_of in cuts:
        heights = jnp.exp(jax.random.uniform(jax.random.fold_in(own, position), (shards_of,), jnp.float32, smallest / len(cuts), largest / len(cuts)))
        level = level * jnp.repeat(heights, shape[position] // shards_of).reshape([-1 if axis == position else 1 for axis in range(len(shape))])
    return level


def noise(own_key, dims, spread, limit, pieces=(), kind=jnp.bfloat16):
    level = block_levels(own_key, dims, pieces, -0.22, 0.18) if pieces else 1.0
    result = jax.random.normal(own_key, dims, jnp.float32) * spread * level
    return jnp.minimum(jnp.maximum(result, -limit), limit).astype(kind)


def heavy_noise(rng, extent, spread, limit, pieces, heavy, held_as=jnp.bfloat16):
    entries = spread * jax.random.normal(rng, extent, jnp.float32)
    if pieces:
        entries = entries * block_levels(rng, extent, pieces, -0.22, 0.18)
    return jnp.clip(raised(entries, jax.random.fold_in(rng, 3), *heavy), -limit, limit).astype(held_as)


def setup_inputs(seed: int = 0) -> dict:
    key_of = jax.random.split(jax.random.key(seed), 7)
    inputs = noise(key_of[0], (TOKENS, D), 1.0, 6.0, ((0, 8), (1, 4)))
    gate_preact = noise(key_of[1], (TOKENS, FF), 1.0, 6.0, ((0, 8), (1, 4)))
    hidden_grad = heavy_noise(key_of[2], (TOKENS, FF), (TOKENS ** -0.5), 0.15625, ((0, 8), (1, 4)), (0, 1, 8, 2.0))
    projector = noise(key_of[3], (D, RANK), D ** -0.5, 0.0625, ((0, 4),))
    first_moment = noise(key_of[4], (FF, RANK), 0.1, 0.6, ((0, 32),), jnp.float32)
    second_moment = jnp.clip(jnp.exp(math.log(0.1) - 2.3025851 * jax.random.uniform(key_of[5], (FF, RANK), jnp.float32) ** block_levels(key_of[5], (FF, RANK), ((0, 32),), -0.2, 0.2)), 0.01, 0.1)
    return {"inputs": inputs, "gate_preact": gate_preact, "hidden_grad": hidden_grad, "projector": projector, "first_moment": first_moment, "second_moment": second_moment}


def reference(inputs, gate_preact, hidden_grad, projector, first_moment, second_moment):
    grad_up = (hidden_grad.astype(jnp.float32) * jax.nn.silu(gate_preact.astype(jnp.float32))).astype(jnp.bfloat16)
    coords = jnp.dot(inputs, projector, preferred_element_type=jnp.float32).astype(jnp.bfloat16)
    projected = jnp.dot(grad_up.T, coords, preferred_element_type=jnp.float32)
    new_first = 0.9 * first_moment + 0.1 * projected
    new_second = 0.95 * second_moment + 0.05 * projected * projected
    direction = new_first / (1.0 - 0.81) / (jnp.sqrt(new_second / (1.0 - 0.9025)) + 1e-08)
    direction = direction.astype(jnp.bfloat16)
    update = 4.0 * jnp.dot(direction, projector.T, preferred_element_type=jnp.float32)
    return (new_first, new_second, update.astype(jnp.bfloat16))
```

```python
import functools

import jax
import jax.numpy as jnp
from jax import lax
from jax.experimental import pallas as pl
from jax.experimental.pallas import tpu as pltpu
from jax.sharding import PartitionSpec as P

MESH = pl.DeviceIdType.MESH
F32 = jnp.float32
BF16 = jnp.bfloat16


def dot_t(a, b):
    return lax.dot_general(a, b, (((0,), (0,)), ((), ())), preferred_element_type=F32)


def exchange_kernel(
    cfg, x_hbm, gate_hbm, hg_hbm, p_hbm, out_ref, pfull,
    xin, pin, gbuf, hbuf, gs, go, gr, ps, ru, rd, cpart, c1s, c1r, co, acc_ref,
    lsem, gsem, hsem, xs, xr, zs, zu, zd,
    s1s, s1r, s2s, s2r, sxs, sxr, s3s, s3r, sib_s, sib_r, pgs, pgr, pfs, pfr,
):
    n, mp, f, cw, pieces, sliced = cfg
    chunks = f // cw
    dp = lax.axis_index("dp")
    m = lax.axis_index("mp")
    z, x = dp // 2, dp % 2
    xp = dp + 1 - 2 * x
    core = m % 2
    sib = m + 1 - 2 * core
    chip = m // 2
    nch = mp // 2
    rows = co.shape[1] // mp
    pr = p_hbm.shape[0]
    pc_rows = pr // pieces

    def peer(o):
        return lax.rem(m + o, mp)

    def source(o):
        return lax.rem(m + mp - o, mp)

    def blocks(fn_up, fn_down, fn_own):
        @pl.loop(0, n - 1)
        def _(k):
            @pl.when(k >= z)
            def _():
                fn_up(n - 1 - k + z)

            @pl.when(k >= n - 1 - z)
            def _():
                fn_down(k - (n - 1 - z))

        if fn_own is not None:
            fn_own(z)

    def cols(ref, d):
        if sliced:
            return ref.at[:, pl.ds(pl.multiple_of(d * f, 128), f)]
        return ref.at[d]

    def load(side, t):
        d = 2 * t + (x if side else 1 - x)
        return (
            pltpu.make_async_copy(cols(gate_hbm, d), gbuf.at[side, t], gsem.at[side, t]),
            pltpu.make_async_copy(cols(hg_hbm, d), hbuf.at[side, t], hsem.at[side, t]),
        )

    def start_load(side):
        def go_(t):
            for c in load(side, t):
                c.start()
        return go_

    in_copy = pltpu.make_async_copy(x_hbm, xin, lsem.at[0])
    pin_copy = pltpu.make_async_copy(p_hbm, pin, lsem.at[1])
    my_rows = pl.ds(pl.multiple_of(m * pr, 16), pr)
    pown = pltpu.make_async_copy(p_hbm, pfull.at[my_rows], lsem.at[2])
    in_copy.start()
    pin_copy.start()
    blocks(start_load(0), start_load(0), start_load(0))
    blocks(start_load(1), start_load(1), start_load(1))
    pown.start()

    bar = pltpu.get_barrier_semaphore()
    for o in range(1, mp):
        pl.semaphore_signal(bar, inc=1, device_id=(dp, peer(o)), device_id_type=MESH)
    pl.semaphore_signal(bar, inc=1, device_id=(xp, m), device_id_type=MESH)

    @pl.when(z > 0)
    def _():
        pl.semaphore_signal(bar, inc=1, device_id=(dp - 2, m), device_id_type=MESH)

    @pl.when(z < n - 1)
    def _():
        pl.semaphore_signal(bar, inc=1, device_id=(dp + 2, m), device_id_type=MESH)

    in_copy.wait()
    pin_copy.wait()

    @pl.loop(0, mp)
    def _(q):
        r = pl.ds(pl.multiple_of(q * rows, 16), rows)
        v = jnp.dot(xin[r, :], pin[...], preferred_element_type=F32)
        cpart[q] = v
        c1s[q] = v.astype(BF16)

    neighbours = (z + n - 1) // n + (2 * n - 2 - z) // n
    pl.semaphore_wait(bar, mp + neighbours)

    def rc(src, dst, ss, rs, dev):
        return pltpu.make_async_remote_copy(
            src_ref=src, dst_ref=dst, send_sem=ss, recv_sem=rs, device_id=dev, device_id_type=MESH
        )

    def first(o):
        return rc(c1s.at[peer(o)], c1r.at[o - 1], s1s.at[o - 1], s1r.at[o - 1], (dp, peer(o)))

    for o in range(1, mp):
        first(o).start()

    def grad(side, t, c):
        sl = pl.ds(pl.multiple_of(c * cw, 128), cw) if chunks > 1 else slice(None)
        v = gbuf[side, t, :, sl].astype(F32)
        h = 0.5 * v
        silu = h + h * jnp.tanh(h)
        return (hbuf[side, t, :, sl].astype(F32) * silu).astype(BF16)

    def xcopy(t, c):
        return rc(gs.at[t, c], gr.at[t, c], xs.at[t, c], xr.at[t, c], (xp, m))

    def send_grads(t):
        for c in load(0, t):
            c.wait()

        @pl.loop(0, chunks)
        def _(c):
            gs[t, c] = grad(0, t, c)
            xcopy(t, c).start()

    def own_grads(t):
        for c in load(1, t):
            c.wait()

        @pl.loop(0, chunks)
        def _(c):
            go[t, c] = grad(1, t, c)

    blocks(send_grads, send_grads, None)

    def crow(q):
        return pl.ds(pl.multiple_of(q * rows, 16), rows)

    def second(o, q):
        return rc(co.at[0, crow(q)], co.at[0, crow(q)], s2s.at[o - 1], s2r.at[o - 1], (dp, peer(o)))

    def third(o, q):
        return rc(co.at[1, crow(q)], co.at[1, crow(q)], s3s.at[o - 1], s3r.at[o - 1], (dp, peer(o)))

    across = rc(co.at[0, crow(m)], co.at[1, crow(m)], sxs.at[0], sxr.at[0], (xp, m))

    total = cpart[m]
    for o in range(1, mp):
        first(o).wait_recv()
        total = total + c1r[o - 1].astype(F32)
    co[0, crow(m), :] = total.astype(BF16)
    across.start()
    for o in range(1, mp):
        second(o, m).start()

    send_grads(z)
    across.wait_recv()
    for o in range(1, mp):
        third(o, m).start()

    def piece(q, i):
        return pfull.at[pl.ds(pl.multiple_of(q * pr + i * pc_rows, 16), pc_rows)]

    sib_copy = rc(p_hbm, pfull.at[my_rows], sib_s.at[0], sib_r.at[0], (dp, sib))

    def chip_peer(o):
        return lax.rem(chip + o, nch) * 2 + core

    def chip_source(o, c):
        return lax.rem(chip + nch - o, nch) * 2 + c

    def pg(o, i):
        src = p_hbm.at[pl.ds(i * pc_rows, pc_rows)]
        return rc(src, piece(m, i), pgs.at[o - 1, i], pgr.at[o - 1, i], (dp, chip_peer(o)))

    def pg_in(o, i):
        q = chip_source(o, core)
        return rc(piece(q, i), piece(q, i), pgs.at[o - 1, i], pgr.at[o - 1, i], (dp, q))

    def pf(o, i, c):
        q = chip_source(o, c)
        return rc(piece(q, i), piece(q, i), pfs.at[o - 1, i], pfr.at[o - 1, i], (dp, sib))

    for o in range(1, nch):
        for i in range(pieces):
            pg(o, i).start()
    sib_copy.start()

    blocks(own_grads, own_grads, own_grads)
    for o in range(1, mp):
        second(o, source(o)).wait_recv()
        third(o, source(o)).wait_recv()

    def partial(t, c):
        xcopy(t, c).wait_recv()
        return dot_t(go[t, c], co[0]) + dot_t(gr[t, c], co[1])

    def zup(t, c):
        return rc(ps.at[t, c], ru.at[t, c], zs.at[t, c], zu.at[t, c], (dp + 2, m))

    def zdown(t, c):
        return rc(ps.at[t, c], rd.at[t, c], zs.at[t, c], zd.at[t, c], (dp - 2, m))

    def zup_in(t, c):
        return rc(ps.at[t, c], ru.at[t, c], zs.at[t, c], zu.at[t, c], (dp - 2, m))

    def zdown_in(t, c):
        return rc(ps.at[t, c], rd.at[t, c], zs.at[t, c], zd.at[t, c], (dp + 2, m))

    def reduce_up(t):
        @pl.loop(0, chunks)
        def _(c):
            acc_ref[...] = partial(t, c)

            @pl.when(z > 0)
            def _():
                zup_in(t, c).wait_recv()
                acc_ref[...] += ru[t, c].astype(F32)

            ps[t, c] = acc_ref[...].astype(BF16)
            zup(t, c).start()

    def reduce_down(t):
        @pl.loop(0, chunks)
        def _(c):
            acc_ref[...] = partial(t, c)

            @pl.when(z < n - 1)
            def _():
                zdown_in(t, c).wait_recv()
                acc_ref[...] += rd[t, c].astype(F32)

            ps[t, c] = acc_ref[...].astype(BF16)
            zdown(t, c).start()

    blocks(reduce_up, reduce_down, None)

    def orow(c):
        return pl.ds(pl.multiple_of(c * cw, 16), cw)

    @pl.loop(0, chunks)
    def _(c):
        out_ref[orow(c), :] = partial(z, c)

    for o in range(1, nch):
        for i in range(pieces):
            pg_in(o, i).wait_recv()
            pf(o, i, core).start()

    @pl.loop(0, chunks)
    def _(c):
        @pl.when(z > 0)
        def _():
            zup_in(z, c).wait_recv()
            out_ref[orow(c), :] += ru[z, c].astype(F32)

        @pl.when(z < n - 1)
        def _():
            zdown_in(z, c).wait_recv()
            out_ref[orow(c), :] += rd[z, c].astype(F32)

    pown.wait()
    sib_copy.wait_send()
    rc(p_hbm, pfull.at[pl.ds(pl.multiple_of(sib * pr, 16), pr)],
       sib_s.at[0], sib_r.at[0], (dp, sib)).wait_recv()
    for o in range(1, nch):
        for i in range(pieces):
            pg(o, i).wait_send()
            pf(o, i, core).wait_send()
            pf(o, i, 1 - core).wait_recv()
    across.wait_send()
    for o in range(1, mp):
        first(o).wait_send()
        second(o, m).wait_send()
        third(o, m).wait_send()

    def finish_x(t):
        @pl.loop(0, chunks)
        def _(c):
            xcopy(t, c).wait_send()

    def finish_up(t):
        finish_x(t)

        @pl.loop(0, chunks)
        def _(c):
            zup(t, c).wait_send()

    def finish_down(t):
        finish_x(t)

        @pl.loop(0, chunks)
        def _(c):
            zdown(t, c).wait_send()

    blocks(finish_up, finish_down, finish_x)


def adam_kernel(proj_ref, m_ref, v_ref, p_ref, nm_ref, nv_ref, u_ref, d_ref):
    @pl.when(pl.program_id(0) == 0)
    def _():
        g = proj_ref[...]
        nm = 0.9 * m_ref[...] + 0.1 * g
        nv = 0.95 * v_ref[...] + 0.05 * g * g
        nm_ref[...] = nm
        nv_ref[...] = nv
        d = nm / (1.0 - 0.81) / (jnp.sqrt(nv / (1.0 - 0.9025)) + 1e-08)
        d_ref[...] = d.astype(BF16)

    u = lax.dot_general(
        d_ref[...], p_ref[...], (((1,), (1,)), ((), ())), preferred_element_type=F32
    )
    u_ref[...] = (4.0 * u).astype(BF16)


def local(ndp, mp, inputs, gate, hg, projector, first_moment, second_moment):
    tok, dl = inputs.shape
    units = gate.shape[1]
    pr, rank = projector.shape
    n = ndp // 2
    f = units // ndp
    sliced = f % 128 == 0
    cw = 128 if sliced else f
    chunks = f // cw
    pieces = 4
    if not sliced:
        gate = gate.reshape(tok, ndp, f).transpose(1, 0, 2)
        hg = hg.reshape(tok, ndp, f).transpose(1, 0, 2)
    rows = tok // mp
    any_ = pl.BlockSpec(memory_space=pl.ANY)
    dma = pltpu.SemaphoreType.DMA
    nch1 = max(mp // 2 - 1, 1)
    projected, pfull = pl.pallas_call(
        functools.partial(exchange_kernel, (n, mp, f, cw, pieces, sliced)),
        out_shape=(
            jax.ShapeDtypeStruct((f, rank), F32),
            jax.ShapeDtypeStruct((pr * mp, rank), BF16),
        ),
        in_specs=[any_] * 4,
        out_specs=(pl.BlockSpec(memory_space=pltpu.VMEM), any_),
        scratch_shapes=[
            pltpu.VMEM((tok, dl), BF16),
            pltpu.VMEM((pr, rank), BF16),
            pltpu.VMEM((2, n, tok, f), BF16),
            pltpu.VMEM((2, n, tok, f), BF16),
            pltpu.VMEM((n, chunks, tok, cw), BF16),
            pltpu.VMEM((n, chunks, tok, cw), BF16),
            pltpu.VMEM((n, chunks, tok, cw), BF16),
            pltpu.VMEM((n, chunks, cw, rank), BF16),
            pltpu.VMEM((n, chunks, cw, rank), BF16),
            pltpu.VMEM((n, chunks, cw, rank), BF16),
            pltpu.VMEM((mp, rows, rank), F32),
            pltpu.VMEM((mp, rows, rank), BF16),
            pltpu.VMEM((mp - 1, rows, rank), BF16),
            pltpu.VMEM((2, tok, rank), BF16),
            pltpu.VMEM((cw, rank), F32),
            dma((3,)),
            dma((2, n)), dma((2, n)),
            dma((n, chunks)), dma((n, chunks)),
            dma((n, chunks)), dma((n, chunks)), dma((n, chunks)),
            dma((mp - 1,)), dma((mp - 1,)),
            dma((mp - 1,)), dma((mp - 1,)),
            dma((1,)), dma((1,)),
            dma((mp - 1,)), dma((mp - 1,)),
            dma((1,)), dma((1,)),
            dma((nch1, pieces)), dma((nch1, pieces)),
            dma((nch1, pieces)), dma((nch1, pieces)),
        ],
        compiler_params=pltpu.CompilerParams(
            collective_id=0, has_side_effects=True, vmem_limit_bytes=56 * 2**20
        ),
        cost_estimate=pl.CostEstimate(
            flops=2 * tok * dl * rank + 2 * tok * units * rank,
            bytes_accessed=4 * tok * units + 2 * tok * dl + 2 * pr * rank * mp,
            transcendentals=tok * units,
        ),
        name="exchange",
    )(inputs, gate, hg, projector)

    d = pr * mp
    bw = 1024 if d % 1024 == 0 else d
    full = pl.BlockSpec((f, rank), lambda i: (0, 0))
    return pl.pallas_call(
        adam_kernel,
        grid=(d // bw,),
        out_shape=(
            jax.ShapeDtypeStruct((f, rank), F32),
            jax.ShapeDtypeStruct((f, rank), F32),
            jax.ShapeDtypeStruct((f, d), BF16),
        ),
        in_specs=[full, full, full, pl.BlockSpec((bw, rank), lambda i: (i, 0))],
        out_specs=(full, full, pl.BlockSpec((f, bw), lambda i: (0, i))),
        scratch_shapes=[pltpu.VMEM((f, rank), BF16)],
        compiler_params=pltpu.CompilerParams(vmem_limit_bytes=48 * 2**20),
        name="update",
    )(projected, first_moment, second_moment, pfull)


def solution(mesh):
    return jax.shard_map(
        functools.partial(local, mesh.shape["dp"], mesh.shape["mp"]),
        mesh=mesh,
        in_specs=(
            P("dp", "mp"),
            P("dp", "mp"),
            P("dp", "mp"),
            P("mp", None),
            P(("mp", "dp"), None),
            P(("mp", "dp"), None),
        ),
        out_specs=(P(("mp", "dp"), None), P(("mp", "dp"), None), P(("mp", "dp"), None)),
        check_vma=False,
    )
```

```python
import functools

import jax
import jax.numpy as jnp
from jax import lax
from jax.experimental import pallas as pl
from jax.experimental.pallas import tpu as pltpu
from jax.sharding import PartitionSpec as P

MESH = pl.DeviceIdType.MESH
F32 = jnp.float32
BF16 = jnp.bfloat16


def dot_t(a, b):
    return lax.dot_general(a, b, (((0,), (0,)), ((), ())), preferred_element_type=F32)


def exchange_kernel(
    cfg, x_hbm, gate_hbm, hg_hbm, p_hbm, out_ref, pfull,
    xin, pin, gbuf, hbuf, gs, go, gr, ps, ru, rd, cpart, c1s, c1r, co, acc_ref,
    lsem, gsem, hsem, xs, xr, zs, zu, zd,
    s1s, s1r, s2s, s2r, sxs, sxr, s3s, s3r, sib_s, sib_r, pgs, pgr, pfs, pfr,
):
    n, mp, f, cw, pieces, sliced = cfg
    chunks = f // cw
    dp = lax.axis_index("dp")
    m = lax.axis_index("mp")
    z, x = dp // 2, dp % 2
    xp = dp + 1 - 2 * x
    core = m % 2
    sib = m + 1 - 2 * core
    chip = m // 2
    nch = mp // 2
    rows = co.shape[1] // mp
    pr = p_hbm.shape[0]
    pc_rows = pr // pieces

    def peer(o):
        return lax.rem(m + o, mp)

    def source(o):
        return lax.rem(m + mp - o, mp)

    def blocks(fn_up, fn_down, fn_own):
        @pl.loop(0, n - 1)
        def _(k):
            @pl.when(k >= z)
            def _():
                fn_up(n - 1 - k + z)

            @pl.when(k >= n - 1 - z)
            def _():
                fn_down(k - (n - 1 - z))

        if fn_own is not None:
            fn_own(z)

    def cols(ref, d):
        if sliced:
            return ref.at[:, pl.ds(pl.multiple_of(d * f, 128), f)]
        return ref.at[d]

    def load(side, t):
        d = 2 * t + (x if side else 1 - x)
        return (
            pltpu.make_async_copy(cols(gate_hbm, d), gbuf.at[side, t], gsem.at[side, t]),
            pltpu.make_async_copy(cols(hg_hbm, d), hbuf.at[side, t], hsem.at[side, t]),
        )

    def start_load(side):
        def go_(t):
            for c in load(side, t):
                c.start()
        return go_

    in_copy = pltpu.make_async_copy(x_hbm, xin, lsem.at[0])
    pin_copy = pltpu.make_async_copy(p_hbm, pin, lsem.at[1])
    my_rows = pl.ds(pl.multiple_of(m * pr, 16), pr)
    pown = pltpu.make_async_copy(pin, pfull.at[my_rows], lsem.at[2])
    in_copy.start()
    pin_copy.start()
    blocks(start_load(0), start_load(0), start_load(0))
    blocks(start_load(1), start_load(1), start_load(1))

    bar = pltpu.get_barrier_semaphore()
    for o in range(1, mp):
        pl.semaphore_signal(bar, inc=1, device_id=(dp, peer(o)), device_id_type=MESH)
    pl.semaphore_signal(bar, inc=1, device_id=(xp, m), device_id_type=MESH)

    @pl.when(z > 0)
    def _():
        pl.semaphore_signal(bar, inc=1, device_id=(dp - 2, m), device_id_type=MESH)

    @pl.when(z < n - 1)
    def _():
        pl.semaphore_signal(bar, inc=1, device_id=(dp + 2, m), device_id_type=MESH)

    in_copy.wait()
    pin_copy.wait()
    pown.start()

    @pl.loop(0, mp)
    def _(q):
        r = pl.ds(pl.multiple_of(q * rows, 16), rows)
        v = jnp.dot(xin[r, :], pin[...], preferred_element_type=F32)
        cpart[q] = v
        c1s[q] = v.astype(BF16)

    neighbours = (z + n - 1) // n + (2 * n - 2 - z) // n
    pl.semaphore_wait(bar, mp + neighbours)

    def rc(src, dst, ss, rs, dev):
        return pltpu.make_async_remote_copy(
            src_ref=src, dst_ref=dst, send_sem=ss, recv_sem=rs, device_id=dev, device_id_type=MESH
        )

    def first(o):
        return rc(c1s.at[peer(o)], c1r.at[o - 1], s1s.at[o - 1], s1r.at[o - 1], (dp, peer(o)))

    for o in range(1, mp):
        first(o).start()

    def grad(side, t, c):
        sl = pl.ds(pl.multiple_of(c * cw, 128), cw) if chunks > 1 else slice(None)
        v = gbuf[side, t, :, sl].astype(F32)
        h = 0.5 * v
        silu = h + h * jnp.tanh(h)
        return (hbuf[side, t, :, sl].astype(F32) * silu).astype(BF16)

    def xcopy(t, c):
        return rc(gs.at[t, c], gr.at[t, c], xs.at[t, c], xr.at[t, c], (xp, m))

    def send_grads(t):
        for c in load(0, t):
            c.wait()

        @pl.loop(0, chunks)
        def _(c):
            gs[t, c] = grad(0, t, c)

    def own_grads(t):
        for c in load(1, t):
            c.wait()

        @pl.loop(0, chunks)
        def _(c):
            go[t, c] = grad(1, t, c)

    upper = 2 * z // n
    lead = (1 - 2 * upper) * (n - 1 - 2 * z)

    def order(j):
        alone = (lead + n - 1 - j) // n
        r = (j - lead) * (1 - alone)
        half, odd = r // 2, r % 2
        low = alone * (n - 1 - j) + (1 - alone) * ((1 - odd) * (2 * z - half) + odd * half)
        high = alone * j + (1 - alone) * ((1 - odd) * (n - 1 - half) + odd * (lead + half))
        return (1 - upper) * low + upper * high

    send_grads(order(0))

    @pl.loop(0, chunks)
    def _(c):
        xcopy(order(0), c).start()

    def crow(q):
        return pl.ds(pl.multiple_of(q * rows, 16), rows)

    def second(o, q):
        return rc(co.at[0, crow(q)], co.at[0, crow(q)], s2s.at[o - 1], s2r.at[o - 1], (dp, peer(o)))

    def third(o, q):
        return rc(co.at[1, crow(q)], co.at[1, crow(q)], s3s.at[o - 1], s3r.at[o - 1], (dp, peer(o)))

    across = rc(co.at[0, crow(m)], co.at[1, crow(m)], sxs.at[0], sxr.at[0], (xp, m))

    total = cpart[m]
    for o in range(1, mp):
        first(o).wait_recv()
        total = total + c1r[o - 1].astype(F32)
    co[0, crow(m), :] = total.astype(BF16)
    across.start()
    for o in range(1, mp):
        second(o, m).start()

    @pl.loop(1, n)
    def _(j):
        send_grads(order(j))

    across.wait_recv()
    for o in range(1, mp):
        third(o, m).start()

    def piece(q, i):
        return pfull.at[pl.ds(pl.multiple_of(q * pr + i * pc_rows, 16), pc_rows)]

    sib_copy = rc(p_hbm, pfull.at[my_rows], sib_s.at[0], sib_r.at[0], (dp, sib))

    def chip_peer(o):
        return lax.rem(chip + o, nch) * 2 + core

    def chip_source(o, c):
        return lax.rem(chip + nch - o, nch) * 2 + c

    def pg(o, i):
        src = p_hbm.at[pl.ds(i * pc_rows, pc_rows)]
        return rc(src, piece(m, i), pgs.at[o - 1, i], pgr.at[o - 1, i], (dp, chip_peer(o)))

    def pg_in(o, i):
        q = chip_source(o, core)
        return rc(piece(q, i), piece(q, i), pgs.at[o - 1, i], pgr.at[o - 1, i], (dp, q))

    def pf(o, i, c):
        q = chip_source(o, c)
        return rc(piece(q, i), piece(q, i), pfs.at[o - 1, i], pfr.at[o - 1, i], (dp, sib))

    for o in range(1, nch):
        for i in range(pieces):
            pg(o, i).start()
    sib_copy.start()

    blocks(own_grads, own_grads, own_grads)
    for o in range(1, mp):
        second(o, source(o)).wait_recv()
        third(o, source(o)).wait_recv()

    def partial(t, c, following=None):
        xcopy(t, c).wait_recv()
        if following is not None:
            xcopy(following, c).start()
        return dot_t(go[t, c], co[0]) + dot_t(gr[t, c], co[1])

    def zup(t, c):
        return rc(ps.at[t, c], ru.at[t, c], zs.at[t, c], zu.at[t, c], (dp + 2, m))

    def zdown(t, c):
        return rc(ps.at[t, c], rd.at[t, c], zs.at[t, c], zd.at[t, c], (dp - 2, m))

    def zup_in(t, c):
        return rc(ps.at[t, c], ru.at[t, c], zs.at[t, c], zu.at[t, c], (dp - 2, m))

    def zdown_in(t, c):
        return rc(ps.at[t, c], rd.at[t, c], zs.at[t, c], zd.at[t, c], (dp + 2, m))

    def reduce_up(t, following):
        @pl.loop(0, chunks)
        def _(c):
            acc_ref[...] = partial(t, c, following)

            @pl.when(z > 0)
            def _():
                zup_in(t, c).wait_recv()
                acc_ref[...] += ru[t, c].astype(F32)

            ps[t, c] = acc_ref[...].astype(BF16)
            zup(t, c).start()

    def reduce_down(t, following):
        @pl.loop(0, chunks)
        def _(c):
            acc_ref[...] = partial(t, c, following)

            @pl.when(z < n - 1)
            def _():
                zdown_in(t, c).wait_recv()
                acc_ref[...] += rd[t, c].astype(F32)

            ps[t, c] = acc_ref[...].astype(BF16)
            zdown(t, c).start()

    @pl.loop(0, n - 1)
    def _(j):
        t, following = order(j), order(j + 1)

        @pl.when(t > z)
        def _():
            reduce_up(t, following)

        @pl.when(t < z)
        def _():
            reduce_down(t, following)

    def orow(c):
        return pl.ds(pl.multiple_of(c * cw, 16), cw)

    @pl.loop(0, chunks)
    def _(c):
        out_ref[orow(c), :] = partial(z, c)

    for o in range(1, nch):
        for i in range(pieces):
            pg_in(o, i).wait_recv()
            pf(o, i, core).start()

    @pl.loop(0, chunks)
    def _(c):
        @pl.when(z > 0)
        def _():
            zup_in(z, c).wait_recv()
            out_ref[orow(c), :] += ru[z, c].astype(F32)

        @pl.when(z < n - 1)
        def _():
            zdown_in(z, c).wait_recv()
            out_ref[orow(c), :] += rd[z, c].astype(F32)

    pown.wait()
    sib_copy.wait_send()
    rc(p_hbm, pfull.at[pl.ds(pl.multiple_of(sib * pr, 16), pr)],
       sib_s.at[0], sib_r.at[0], (dp, sib)).wait_recv()
    for o in range(1, nch):
        for i in range(pieces):
            pg(o, i).wait_send()
            pf(o, i, core).wait_send()
            pf(o, i, 1 - core).wait_recv()
    across.wait_send()
    for o in range(1, mp):
        first(o).wait_send()
        second(o, m).wait_send()
        third(o, m).wait_send()

    def finish_x(t):
        @pl.loop(0, chunks)
        def _(c):
            xcopy(t, c).wait_send()

    def finish_up(t):
        finish_x(t)

        @pl.loop(0, chunks)
        def _(c):
            zup(t, c).wait_send()

    def finish_down(t):
        finish_x(t)

        @pl.loop(0, chunks)
        def _(c):
            zdown(t, c).wait_send()

    blocks(finish_up, finish_down, finish_x)


def adam_kernel(proj_ref, m_ref, v_ref, p_ref, nm_ref, nv_ref, u_ref, d_ref):
    @pl.when(pl.program_id(0) == 0)
    def _():
        g = proj_ref[...]
        nm = 0.9 * m_ref[...] + 0.1 * g
        nv = 0.95 * v_ref[...] + 0.05 * g * g
        nm_ref[...] = nm
        nv_ref[...] = nv
        d = nm / (1.0 - 0.81) / (jnp.sqrt(nv / (1.0 - 0.9025)) + 1e-08)
        d_ref[...] = d.astype(BF16)

    u = lax.dot_general(
        d_ref[...], p_ref[...], (((1,), (1,)), ((), ())), preferred_element_type=F32
    )
    u_ref[...] = (4.0 * u).astype(BF16)


def local(ndp, mp, inputs, gate, hg, projector, first_moment, second_moment):
    tok, dl = inputs.shape
    units = gate.shape[1]
    pr, rank = projector.shape
    n = ndp // 2
    f = units // ndp
    sliced = f % 128 == 0
    cw = 128 if sliced else f
    chunks = f // cw
    pieces = 4
    if not sliced:
        gate = gate.reshape(tok, ndp, f).transpose(1, 0, 2)
        hg = hg.reshape(tok, ndp, f).transpose(1, 0, 2)
    rows = tok // mp
    any_ = pl.BlockSpec(memory_space=pl.ANY)
    dma = pltpu.SemaphoreType.DMA
    nch1 = max(mp // 2 - 1, 1)
    projected, pfull = pl.pallas_call(
        functools.partial(exchange_kernel, (n, mp, f, cw, pieces, sliced)),
        out_shape=(
            jax.ShapeDtypeStruct((f, rank), F32),
            jax.ShapeDtypeStruct((pr * mp, rank), BF16),
        ),
        in_specs=[any_] * 4,
        out_specs=(pl.BlockSpec(memory_space=pltpu.VMEM), any_),
        scratch_shapes=[
            pltpu.VMEM((tok, dl), BF16),
            pltpu.VMEM((pr, rank), BF16),
            pltpu.VMEM((2, n, tok, f), BF16),
            pltpu.VMEM((2, n, tok, f), BF16),
            pltpu.VMEM((n, chunks, tok, cw), BF16),
            pltpu.VMEM((n, chunks, tok, cw), BF16),
            pltpu.VMEM((n, chunks, tok, cw), BF16),
            pltpu.VMEM((n, chunks, cw, rank), BF16),
            pltpu.VMEM((n, chunks, cw, rank), BF16),
            pltpu.VMEM((n, chunks, cw, rank), BF16),
            pltpu.VMEM((mp, rows, rank), F32),
            pltpu.VMEM((mp, rows, rank), BF16),
            pltpu.VMEM((mp - 1, rows, rank), BF16),
            pltpu.VMEM((2, tok, rank), BF16),
            pltpu.VMEM((cw, rank), F32),
            dma((3,)),
            dma((2, n)), dma((2, n)),
            dma((n, chunks)), dma((n, chunks)),
            dma((n, chunks)), dma((n, chunks)), dma((n, chunks)),
            dma((mp - 1,)), dma((mp - 1,)),
            dma((mp - 1,)), dma((mp - 1,)),
            dma((1,)), dma((1,)),
            dma((mp - 1,)), dma((mp - 1,)),
            dma((1,)), dma((1,)),
            dma((nch1, pieces)), dma((nch1, pieces)),
            dma((nch1, pieces)), dma((nch1, pieces)),
        ],
        compiler_params=pltpu.CompilerParams(
            collective_id=0, has_side_effects=True, vmem_limit_bytes=56 * 2**20
        ),
        cost_estimate=pl.CostEstimate(
            flops=2 * tok * dl * rank + 2 * tok * units * rank,
            bytes_accessed=4 * tok * units + 2 * tok * dl + 2 * pr * rank * mp,
            transcendentals=tok * units,
        ),
        name="exchange",
    )(inputs, gate, hg, projector)

    d = pr * mp
    bw = 1024 if d % 1024 == 0 else d
    full = pl.BlockSpec((f, rank), lambda i: (0, 0))
    return pl.pallas_call(
        adam_kernel,
        grid=(d // bw,),
        out_shape=(
            jax.ShapeDtypeStruct((f, rank), F32),
            jax.ShapeDtypeStruct((f, rank), F32),
            jax.ShapeDtypeStruct((f, d), BF16),
        ),
        in_specs=[full, full, full, pl.BlockSpec((bw, rank), lambda i: (i, 0))],
        out_specs=(full, full, pl.BlockSpec((f, bw), lambda i: (0, i))),
        scratch_shapes=[pltpu.VMEM((f, rank), BF16)],
        compiler_params=pltpu.CompilerParams(vmem_limit_bytes=48 * 2**20),
        name="update",
    )(projected, first_moment, second_moment, pfull)


def solution(mesh):
    return jax.shard_map(
        functools.partial(local, mesh.shape["dp"], mesh.shape["mp"]),
        mesh=mesh,
        in_specs=(
            P("dp", "mp"),
            P("dp", "mp"),
            P("dp", "mp"),
            P("mp", None),
            P(("mp", "dp"), None),
            P(("mp", "dp"), None),
        ),
        out_specs=(P(("mp", "dp"), None), P(("mp", "dp"), None), P(("mp", "dp"), None)),
        check_vma=False,
    )
```
